32 devices in a mesh: expert: 8 (over z, y), dp: 4 (over x, core).
Axes of the slice: x: 2, y: 2, z: 4, core: 2. Of those that a mesh axis runs over, the one named last changes fastest.
Arguments:
- cotangent: bfloat16 [4096, 2048], P(('expert', 'dp')), may hold values from -4 to 4
- router_probs: bfloat16 [4096, 1], P(('expert', 'dp')), may hold values from 0.049804688 to 0.59765625
- slot_ids: int32 [4096, 1], P(('expert', 'dp')), may hold values from 0 to 7; in each aligned block of 128 rows (0 to 127, 128 to 255, ...) at most 24 rows name the same one
- saved_hidden: bfloat16 [8, 768, 1024], P('expert', 'dp'), may hold values from -6 to 6
- down_weight: bfloat16 [8, 2048, 512], P('expert', 'dp'), as said below
Outputs:
- grad_down: float32 [8, 2048, 512], P('expert', 'dp')
- grad_hidden: bfloat16 [8, 768, 1024], P('expert', 'dp')
- grad_probs: float32 [4096, 1], P(('expert', 'dp'))
The draws below stay inside these ranges and needn't reach their ends.
Inputs may be any that keep to these rules, and one draw needn't show every extreme that they name: `slot_ids`: in the 128 tokens of one device, each token names one slot, no slot is named by more than 24 tokens, a bound that some block reaches. `down_weight`: slots s and s + 4 hold the same expert's weights.
All inputs are finite; a program needn't handle non-finite values.
Results may differ from the reference program's by a relative error of at most 0.007.
Values may be sent and summed in bfloat16 or wider, within the bound.
A program may use at most 64 MiB of HBM per device.

```python
import math
import jax
import jax.numpy as jnp
import numpy as np
from jax import lax

D = 2048
FF = 512
TOP = 1
TOK_DEV = 128
EXPERTS = 4
SLOTS = 8
CAP = 24
ROWS = 768
TOKENS = 4096
N_EXPERT = 8
N_DP = 4
DEVICES = 32


def draw_down_weight(key, part):
    base_weight = jax.random.normal(jax.random.fold_in(key, 17), (EXPERTS, D, FF), jnp.float32) * FF ** (-0.5)
    return jnp.concatenate([base_weight, base_weight], axis=0).astype(jnp.bfloat16)


def steps_of(stream_key, dims, split, smallest, high):
    gain, own = 1.0, jax.random.fold_in(stream_key, 6)
    for dim, shards_of in split:
        steps = jnp.exp(jax.random.uniform(jax.random.fold_in(own, dim), (shards_of,), jnp.float32, smallest / len(split), high / len(split)))
        gain = gain * jnp.repeat(steps, dims[dim] // shards_of).reshape([-1 if axis == dim else 1 for axis in range(len(dims))])
    return gain


def routed_block(own_key, own, number, rows, count, top, reach, lean):
    ranking = jax.random.permutation(own_key, count)
    heavy_load, ordinary = shares(count, rows * top, reach, lean, True), shares(count, rows * top, reach, lean, False)
    places = jnp.arange(count)

    def named(tallies, offset_by):
        used = int((tallies > 0).sum())
        fixed = max(1, used // 4)
        moved = fixed + (places - fixed + offset_by * (used - fixed)) % max(1, count - fixed)
        return jnp.zeros((count,), jnp.int32).at[ranking[jnp.where(places < fixed, places, moved)]].set(jnp.asarray(tallies, jnp.int32))

    tallies = jnp.where(number % 4 == 0, named(heavy_load, number // 4), named(ordinary, number - number // 4 - 1))
    mixed = jax.random.permutation(jax.random.fold_in(own, 3), count)
    giver, receiver = mixed[0:count // 2 * 2:2], mixed[1:count // 2 * 2:2]
    margin = jnp.minimum(tallies[giver] - 1, reach - tallies[receiver]) // 2
    margin = jnp.where((giver == ranking[0]) | (receiver == ranking[0]) | (tallies[receiver] == 0), 0, jnp.maximum(margin, 0))
    moved = jax.random.randint(jax.random.fold_in(own, 4), (count // 2,), 0, 1 << 20) % (margin + 1)
    tallies = tallies.at[giver].add(-moved).at[receiver].add(moved)
    labels = jnp.searchsorted(jnp.cumsum(tallies), jnp.arange(rows * top), side="right").astype(jnp.int32)
    grid = labels.reshape(top, rows).T
    grid = grid[jax.random.permutation(jax.random.fold_in(own, 1), rows)]
    offset_by = jax.random.randint(jax.random.fold_in(own, 2), (rows, 1), 0, top)
    return jnp.take_along_axis(grid, (jnp.arange(top)[None, :] + offset_by) % top, axis=1)


def shares(count, total, limit, slope, full):
    weights = [(1 << 20) // math.isqrt(rank ** slope) + 1 for rank in range(1, count + 1)]
    largest = limit if full else min(limit, max(-(-total // count), total * weights[0] // sum(weights)))
    least = 1 if total - largest >= count - 1 else 0
    given, surplus = [largest] + [least] * (count - 1), total - largest - least * (count - 1)
    while surplus > 0:
        free = [i for i in range(1, count) if given[i] < largest] or [i for i in range(1, count) if given[i] < limit]
        mass, remaining = sum([weights[i] for i in free]), surplus
        for i in free:
            extra = min(limit - given[i], max(1, remaining * weights[i] // mass), surplus)
            given[i] = given[i] + extra
            surplus = surplus - extra
    return np.array(given)


def normal_values(rng, extent, spread, most, cuts=(), kind=jnp.bfloat16):
    array = spread * jax.random.normal(rng, extent, jnp.float32)
    if cuts:
        array = array * steps_of(rng, extent, cuts, -0.22, 0.18)
    return jnp.clip(array, -most, most).astype(kind)


def setup_inputs(seed: int = 0) -> dict:
    key_of = jax.random.split(jax.random.key(seed), 6)
    cotangent = normal_values(key_of[0], (TOKENS, D), 0.25, 4.0, ((0, 32),))
    router_probs = jnp.clip(0.049804688 + 0.54785156 * jax.random.uniform(key_of[1], (TOKENS, TOP), jnp.float32) ** steps_of(key_of[1], (TOKENS, TOP), ((0, 32),), -0.2, 0.2), 0.049804688, 0.59765625).astype(jnp.bfloat16)
    slot_ids_keys = jax.random.split(jax.random.fold_in(key_of[2], 1), TOKENS // TOK_DEV)
    slot_ids_turns = jax.random.permutation(jax.random.fold_in(key_of[2], 3), TOKENS // TOK_DEV)
    slot_ids = jax.vmap(lambda own, number: routed_block(jax.random.fold_in(key_of[2], 2), own, number, TOK_DEV, SLOTS, TOP, CAP, 2))(slot_ids_keys, slot_ids_turns).reshape((TOKENS, TOP))
    saved_hidden = normal_values(key_of[3], (SLOTS, ROWS, 2 * FF), 1.0, 6.0, ((0, 8), (1, 4)))
    down_weight = draw_down_weight(jax.random.fold_in(key_of[5], 71), 0)
    return {"cotangent": cotangent, "router_probs": router_probs, "slot_ids": slot_ids, "saved_hidden": saved_hidden, "down_weight": down_weight}


def reference(cotangent, router_probs, slot_ids, saved_hidden, down_weight):
    pair_count = TOK_DEV * TOP
    dev_slots = slot_ids.reshape(DEVICES, pair_count)
    slot_range = jnp.arange(SLOTS, dtype=jnp.int32)
    slot_hits = (dev_slots[:, :, None] == slot_range[None, None, :]).astype(jnp.int32)
    earlier = jnp.cumsum(slot_hits, axis=1) - slot_hits
    position = jnp.sum(earlier * slot_hits, axis=2).astype(jnp.int32)
    device_ids = jnp.arange(DEVICES, dtype=jnp.int32)
    exp_index = device_ids // N_DP
    dp_index = device_ids % N_DP
    row_index = (dp_index[:, None] * (N_EXPERT * CAP) + exp_index[:, None] * CAP + position).astype(jnp.int32)
    flat_slot = dev_slots.reshape(-1).astype(jnp.int32)
    flat_row = row_index.reshape(-1).astype(jnp.int32)
    flat_place = (flat_slot * ROWS + flat_row).astype(jnp.int32)
    table = jnp.full((SLOTS * ROWS,), -1, dtype=jnp.int32)
    table = table.at[flat_place].set(jnp.arange(TOKENS * TOP, dtype=jnp.int32))
    table = table.reshape(SLOTS, ROWS)
    flat_probs = router_probs.reshape(-1)

    def per_slot(inputs):
        pair_ids, hidden, weight = inputs
        valid = pair_ids >= 0
        safe_ids = jnp.maximum(pair_ids, 0).astype(jnp.int32)
        cot_rows = jnp.where(valid[:, None], cotangent[safe_ids // TOP], jnp.zeros((), cotangent.dtype))
        prob_rows = jnp.where(valid, flat_probs[safe_ids], jnp.zeros((), flat_probs.dtype))
        gate_pre = hidden[:, :FF].astype(jnp.float32)
        up_pre = hidden[:, FF:].astype(jnp.float32)
        gate_sig = jax.nn.sigmoid(gate_pre)
        gate_act = gate_pre * gate_sig
        activation = (gate_act * up_pre).astype(jnp.bfloat16)
        outputs = lax.dot_general(activation, weight, (((1,), (1,)), ((), ())), preferred_element_type=jnp.float32)
        prob_grad = jnp.sum(cot_rows.astype(jnp.float32) * outputs, axis=1)
        scaled = (prob_rows.astype(jnp.float32)[:, None] * cot_rows.astype(jnp.float32)).astype(jnp.bfloat16)
        grad_act = jnp.dot(scaled, weight, preferred_element_type=jnp.float32)
        grad_gate = grad_act * up_pre * gate_sig * (1.0 + gate_pre * (1.0 - gate_sig))
        grad_up = grad_act * gate_act
        grad_hidden = jnp.concatenate([grad_gate, grad_up], axis=1).astype(jnp.bfloat16)
        weight_grad = lax.dot_general(scaled, activation, (((0,), (0,)), ((), ())), preferred_element_type=jnp.float32)
        return weight_grad, grad_hidden, prob_grad

    weight_grads, grad_hidden, prob_grads = lax.map(per_slot, (table, saved_hidden, down_weight))
    grad_down = weight_grads + jnp.roll(weight_grads, EXPERTS, axis=0)
    grad_probs = prob_grads.reshape(-1)[flat_place].reshape(TOKENS, TOP)
    return grad_down, grad_hidden, grad_probs
```

```python
import functools

import jax
import jax.numpy as jnp
import numpy as np
from jax import lax
from jax.experimental import pallas as pl
from jax.experimental.pallas import tpu as pltpu
from jax.sharding import PartitionSpec as P

MESH = pl.DeviceIdType.MESH
F32 = jnp.float32
BF16 = jnp.bfloat16


def kernel(
    E, N, C, cot_ref, prob_ref, slot_ref, hid_ref, w_ref, by_dp_ref, by_e_ref,
    down_ref, hidden_ref, probs_ref,
    send1, got1, act, act_rows, send2, rows, gsend, gpart, psend, ppart, pg, scaled, spread,
    s1s, s1r, as_, ar, s2s, s2r, gs, gr, ps, pr, qs, qr,
):
    e, d = lax.axis_index("expert"), lax.axis_index("dp")
    tok, width = cot_ref.shape
    block = width // N
    ff = act.shape[2]
    NC, EC = N * C, E * C
    half = lax.rem(e + E // 2, E)

    def copy(src, dst, ss, rs, where):
        return pltpu.make_async_remote_copy(
            src_ref=src, dst_ref=dst, send_sem=ss, recv_sem=rs, device_id=where, device_id_type=MESH
        )

    def peers(n, me, body):
        def step(k, carry):
            body(lax.rem(me + k, n))
            return carry

        lax.fori_loop(1, n, step, 0)

    barrier = pltpu.get_barrier_semaphore()
    peers(N, d, lambda j: pl.semaphore_signal(barrier, inc=1, device_id=(e, j), device_id_type=MESH))
    peers(E, e, lambda j: pl.semaphore_signal(barrier, inc=1, device_id=(j, d), device_id_type=MESH))

    slot = slot_ref[...]
    lanes = lax.broadcasted_iota(jnp.int32, (tok, 128), 1)
    hits = jnp.where(lanes == slot, 1.0, 0.0).astype(F32)
    row_i = lax.broadcasted_iota(jnp.int32, (tok, tok), 0)
    col_i = lax.broadcasted_iota(jnp.int32, (tok, tok), 1)
    before = jnp.where(col_i < row_i, 1.0, 0.0).astype(BF16)
    earlier = jnp.dot(before, hits.astype(BF16), preferred_element_type=F32)
    position = jnp.sum(earlier * hits, axis=1, keepdims=True)
    target = slot.astype(F32) * C + position
    target_row = jnp.sum(jnp.where(row_i == col_i, target, 0.0), axis=0, keepdims=True)
    spread[...] = jnp.where(
        lax.broadcasted_iota(jnp.int32, (EC, tok), 0).astype(F32) == target_row, 1.0, 0.0
    ).astype(BF16)
    prob = prob_ref[...].astype(F32)
    scaled[...] = (cot_ref[...].astype(F32) * prob).astype(BF16)

    def piece(j):
        cols = pl.ds(pl.multiple_of(j * block, block), block)
        return jnp.dot(spread[...], scaled[:, cols], preferred_element_type=F32).astype(BF16)

    pl.semaphore_wait(barrier, N - 1 + E - 1)

    def one(j):
        send1[j] = piece(j)
        copy(send1.at[j], got1.at[d], s1s.at[j], s1r.at[d], (e, j)).start()

    peers(N, d, one)
    got1[d] = piece(d)

    gate = hid_ref[:, :ff].astype(F32)
    up = hid_ref[:, ff:].astype(F32)
    act[d] = (gate * jax.nn.sigmoid(gate) * up).astype(BF16)
    peers(N, d, lambda j: copy(act.at[d], act.at[d], as_.at[j], ar.at[d], (e, j)).start())
    peers(N, d, lambda j: copy(send1.at[j], got1.at[j], s1s.at[j], s1r.at[j], (e, j)).wait_recv())

    lane_r = lax.broadcasted_iota(jnp.int32, (NC, N * EC), 1)

    def pick(j):
        return jnp.where(lane_r == by_dp_ref[...] + j * C, 1.0, 0.0).astype(BF16)

    def select(j, ref):
        whole = ref[...].reshape(N * EC, ref.shape[2])
        return jnp.dot(pick(j), whole, preferred_element_type=F32).astype(BF16)

    def two(j):
        send2[j] = select(j, got1)
        copy(send2.at[j], rows.at[e], s2s.at[j], s2r.at[e], (j, d)).start()

    peers(E, e, two)
    rows[e] = select(e, got1)

    peers(N, d, lambda j: copy(act.at[d], act.at[j], as_.at[j], ar.at[j], (e, j)).wait_recv())

    def order(j, carry):
        act_rows[j] = select(j, act)
        return carry

    lax.fori_loop(0, E, order, 0)
    peers(E, e, lambda j: copy(send2.at[j], rows.at[j], s2s.at[j], s2r.at[j], (j, d)).wait_recv())

    parts = psend.shape[0]
    step = block // parts
    lined = act_rows[...].reshape(E * NC, ff)
    for c in range(parts):
        left = rows[:, :, c * step : (c + 1) * step].reshape(E * NC, step)
        grad = lax.dot_general(left, lined, (((0,), (0,)), ((), ())), preferred_element_type=F32)
        down_ref[c * step : (c + 1) * step, :] = grad
        psend[c] = grad.astype(BF16)
        copy(psend.at[c], ppart.at[c], ps.at[c], pr.at[c], (half, d)).start()

    lane_g = lax.broadcasted_iota(jnp.int32, (EC, E * NC), 1)

    def share(j):
        mine = jnp.where(lane_g == by_e_ref[...] + j * C, 1.0, 0.0).astype(BF16)
        ordered = jnp.dot(mine, rows[...].reshape(E * NC, block), preferred_element_type=F32)
        return jnp.dot(ordered.astype(BF16), w_ref[...], preferred_element_type=F32)

    def three(j):
        gsend[j] = share(j).astype(BF16)
        copy(gsend.at[j], gpart.at[d], gs.at[j], gr.at[d], (e, j)).start()

    peers(N, d, three)
    total = share(d)
    peers(N, d, lambda j: copy(gsend.at[j], gpart.at[j], gs.at[j], gr.at[j], (e, j)).wait_recv())
    total = lax.fori_loop(
        1, N, lambda k, t: t + gpart[lax.rem(d + k, N)].astype(F32), total
    )
    gate = hid_ref[:, :ff].astype(F32)
    up = hid_ref[:, ff:].astype(F32)
    sig = jax.nn.sigmoid(gate)
    pg_col = jnp.sum(total * act[d].astype(F32), axis=1, keepdims=True)
    eye = lax.broadcasted_iota(jnp.int32, (EC, EC), 0) == lax.broadcasted_iota(jnp.int32, (EC, EC), 1)
    pg_row = jnp.sum(jnp.where(eye, pg_col, 0.0), axis=0, keepdims=True)
    pg[e] = jnp.broadcast_to(pg_row, (8, EC))
    peers(E, e, lambda j: copy(pg.at[e], pg.at[e], qs.at[j], qr.at[e], (j, d)).start())
    hidden_ref[:, :ff] = (total * up * sig * (1.0 + gate * (1.0 - sig))).astype(BF16)
    hidden_ref[:, ff:] = (total * gate * sig).astype(BF16)

    peers(E, e, lambda j: copy(pg.at[e], pg.at[j], qs.at[j], qr.at[j], (j, d)).wait_recv())
    place = position + (e * C).astype(F32)
    found = lax.broadcasted_iota(jnp.int32, (tok, EC), 1).astype(F32) == place
    probs_ref[...] = (
        lax.fori_loop(
            0,
            E,
            lambda s, t: t
            + jnp.sum(jnp.where(found & (slot == s), pg[s][0:1, :], 0.0), axis=1, keepdims=True),
            jnp.zeros((tok, 1), F32),
        )
        / prob
    )

    for c in range(parts):
        copy(psend.at[c], ppart.at[c], ps.at[c], pr.at[c], (half, d)).wait_recv()
        down_ref[c * step : (c + 1) * step, :] += ppart[c].astype(F32)

    def sent_dp(j):
        copy(send1.at[j], got1.at[d], s1s.at[j], s1r.at[d], (e, j)).wait_send()
        copy(act.at[d], act.at[d], as_.at[j], ar.at[d], (e, j)).wait_send()
        copy(gsend.at[j], gpart.at[d], gs.at[j], gr.at[d], (e, j)).wait_send()

    def sent_e(j):
        copy(send2.at[j], rows.at[e], s2s.at[j], s2r.at[e], (j, d)).wait_send()
        copy(pg.at[e], pg.at[e], qs.at[j], qr.at[e], (j, d)).wait_send()

    peers(N, d, sent_dp)
    peers(E, e, sent_e)
    for c in range(parts):
        copy(psend.at[c], ppart.at[c], ps.at[c], pr.at[c], (half, d)).wait_send()


def on_device(E, N, cotangent, router_probs, slot_ids, saved_hidden, down_weight):
    tok, width = cotangent.shape
    C = 3 * tok // (2 * E)
    NC, EC = N * C, E * C
    block, ff = down_weight.shape[1:]
    parts = max(1, block // 256)
    by_dp = np.array([[j // C * EC + j % C] for j in range(NC)], np.int32)
    by_e = np.array([[i // C * NC + i % C] for i in range(EC)], np.int32)
    dma = pltpu.SemaphoreType.DMA
    vmem = pl.BlockSpec(memory_space=pltpu.VMEM)
    down, hidden, probs = pl.pallas_call(
        functools.partial(kernel, E, N, C),
        out_shape=(
            jax.ShapeDtypeStruct((block, ff), F32),
            jax.ShapeDtypeStruct((EC, 2 * ff), BF16),
            jax.ShapeDtypeStruct((tok, 1), F32),
        ),
        in_specs=[vmem] * 7,
        out_specs=(vmem,) * 3,
        scratch_shapes=[
            pltpu.VMEM((N, EC, block), BF16),
            pltpu.VMEM((N, EC, block), BF16),
            pltpu.VMEM((N, EC, ff), BF16),
            pltpu.VMEM((E, NC, ff), BF16),
            pltpu.VMEM((E, NC, block), BF16),
            pltpu.VMEM((E, NC, block), BF16),
            pltpu.VMEM((N, EC, ff), BF16),
            pltpu.VMEM((N, EC, ff), BF16),
            pltpu.VMEM((parts, block // parts, ff), BF16),
            pltpu.VMEM((parts, block // parts, ff), BF16),
            pltpu.VMEM((E, 8, EC), F32),
            pltpu.VMEM((tok, width), BF16),
            pltpu.VMEM((EC, tok), BF16),
            dma((N,)), dma((N,)), dma((N,)), dma((N,)), dma((E,)), dma((E,)),
            dma((N,)), dma((N,)), dma((parts,)), dma((parts,)), dma((E,)), dma((E,)),
        ],
        compiler_params=pltpu.CompilerParams(
            collective_id=0, has_side_effects=True, vmem_limit_bytes=56 * 2**20
        ),
        name="expert_backward",
    )(cotangent, router_probs, slot_ids, saved_hidden[0], down_weight[0], by_dp, by_e)
    return down[None], hidden[None], probs


def solution(mesh):
    placed = (
        P(("expert", "dp"), None),
        P(("expert", "dp"), None),
        P(("expert", "dp"), None),
        P("expert", "dp", None),
        P("expert", "dp", None),
    )
    return jax.shard_map(
        functools.partial(on_device, mesh.shape["expert"], mesh.shape["dp"]),
        mesh=mesh,
        in_specs=placed,
        out_specs=(P("expert", "dp", None), P("expert", "dp", None), P(("expert", "dp"), None)),
        check_vma=False,
    )
```

```python
import functools

import jax
import jax.numpy as jnp
import numpy as np
from jax import lax
from jax.experimental import pallas as pl
from jax.experimental.pallas import tpu as pltpu
from jax.sharding import PartitionSpec as P

MESH = pl.DeviceIdType.MESH
F32 = jnp.float32
BF16 = jnp.bfloat16


def kernel(
    E, N, C, cot_ref, prob_ref, slot_ref, hid_ref, w_ref, by_dp_ref, by_act_ref, by_e_ref,
    down_ref, hidden_ref, probs_ref,
    send1, got1, act, act_rows, send2, rows, gsend, gpart, psend, ppart, pg, scaled, spread,
    xact, xsend, xpart, s1s, s1r, as_, ar, s2s, s2r, gs, gr, ps, pr, qs, qr, xs, xr,
):
    e, d = lax.axis_index("expert"), lax.axis_index("dp")
    tok, width = cot_ref.shape
    block = width // N
    ff = act.shape[3]
    H = E // 2
    NC, EC, HC = N * C, E * C, H * C
    mine, x = lax.div(e, H), lax.rem(e, H)
    other = lax.rem(e + H, E)
    start = mine * H

    def copy(src, dst, ss, rs, where):
        return pltpu.make_async_remote_copy(
            src_ref=src, dst_ref=dst, send_sem=ss, recv_sem=rs, device_id=where, device_id_type=MESH
        )

    def peers(n, me, body):
        def step(k, carry):
            body(lax.rem(me + k, n))
            return carry

        lax.fori_loop(1, n, step, 0)

    barrier = pltpu.get_barrier_semaphore()
    peers(N, d, lambda j: pl.semaphore_signal(barrier, inc=1, device_id=(e, j), device_id_type=MESH))
    peers(
        H, x,
        lambda j: pl.semaphore_signal(barrier, inc=1, device_id=(start + j, d), device_id_type=MESH),
    )
    pl.semaphore_signal(barrier, inc=1, device_id=(other, d), device_id_type=MESH)

    def half_rows(g):
        return pl.ds(pl.multiple_of(g * HC, HC), HC)

    def activation(g):
        gate = hid_ref[half_rows(g), :ff].astype(F32)
        up = hid_ref[half_rows(g), ff:].astype(F32)
        return (gate * jax.nn.sigmoid(gate) * up).astype(BF16)

    xact[...] = activation(1 - mine)

    slot = slot_ref[...]
    lanes = lax.broadcasted_iota(jnp.int32, (tok, 128), 1)
    hits = jnp.where(lanes == slot, 1.0, 0.0).astype(F32)
    row_i = lax.broadcasted_iota(jnp.int32, (tok, tok), 0)
    col_i = lax.broadcasted_iota(jnp.int32, (tok, tok), 1)
    before = jnp.where(col_i < row_i, 1.0, 0.0).astype(BF16)
    earlier = jnp.dot(before, hits.astype(BF16), preferred_element_type=F32)
    position = jnp.sum(earlier * hits, axis=1, keepdims=True)
    target = slot.astype(F32) * C + position
    target_row = jnp.sum(jnp.where(row_i == col_i, target, 0.0), axis=0, keepdims=True)
    spread[...] = jnp.where(
        lax.broadcasted_iota(jnp.int32, (EC, tok), 0).astype(F32) == target_row, 1.0, 0.0
    ).astype(BF16)
    prob = prob_ref[...].astype(F32)
    scaled[...] = (cot_ref[...].astype(F32) * prob).astype(BF16)

    def piece(j):
        cols = pl.ds(pl.multiple_of(j * block, block), block)
        return jnp.dot(spread[...], scaled[:, cols], preferred_element_type=F32).astype(BF16)

    pl.semaphore_wait(barrier, N - 1 + H)
    cross_act = copy(xact, act.at[1, d], xs.at[0], xr.at[0], (other, d))
    cross_act.start()

    def one(j):
        send1[j] = piece(j)
        copy(send1.at[j], got1.at[d], s1s.at[j], s1r.at[d], (e, j)).start()

    peers(N, d, one)
    got1[d] = piece(d)

    act[0, d] = activation(mine)

    def give(i):
        peers(N, d, lambda j: copy(act.at[i, d], act.at[i, d], as_.at[i, j], ar.at[i, d], (e, j)).start())

    give(0)
    peers(N, d, lambda j: copy(send1.at[j], got1.at[j], s1s.at[j], s1r.at[j], (e, j)).wait_recv())

    lane_r = lax.broadcasted_iota(jnp.int32, (NC, N * EC), 1)

    def select(base, ref):
        pick = jnp.where(lane_r == base, 1.0, 0.0).astype(BF16)
        whole = ref[...].reshape(N * EC, ref.shape[-1])
        return jnp.dot(pick, whole, preferred_element_type=F32).astype(BF16)

    def rows_of(s):
        return select(by_dp_ref[...] + s * C, got1)

    def two(j):
        send2[j, 0] = rows_of(start + j)
        send2[j, 1] = rows_of((1 - mine) * H + j)
        copy(send2.at[j], rows.at[x], s2s.at[j], s2r.at[x], (start + j, d)).start()

    peers(H, x, two)
    cross_act.wait_recv()
    give(1)
    rows[x, 0] = rows_of(e)
    rows[x, 1] = rows_of(other)

    for i in range(2):
        peers(
            N, d,
            lambda j: copy(act.at[i, d], act.at[i, j], as_.at[i, j], ar.at[i, j], (e, j)).wait_recv(),
        )

    def order(j, carry):
        for i in range(2):
            act_rows[j, i] = select(by_act_ref[...] + (i * N * HC + j * C), act)
        return carry

    lax.fori_loop(0, H, order, 0)
    peers(
        H, x,
        lambda j: copy(send2.at[j], rows.at[j], s2s.at[j], s2r.at[j], (start + j, d)).wait_recv(),
    )

    parts = psend.shape[0]
    step = block // parts
    lined = act_rows[...].reshape(E * NC, ff)
    for c in range(parts):
        left = rows[:, :, :, c * step : (c + 1) * step].reshape(E * NC, step)
        grad = lax.dot_general(left, lined, (((0,), (0,)), ((), ())), preferred_element_type=F32)
        down_ref[c * step : (c + 1) * step, :] = grad
        psend[c] = grad.astype(BF16)
        copy(psend.at[c], ppart.at[c], ps.at[c], pr.at[c], (other, d)).start()

    lane_g = lax.broadcasted_iota(jnp.int32, (EC, E * NC), 1)

    def share(j):
        pick = jnp.where(lane_g == by_e_ref[...] + j * C, 1.0, 0.0).astype(BF16)
        ordered = jnp.dot(pick, rows[...].reshape(E * NC, block), preferred_element_type=F32)
        return jnp.dot(ordered.astype(BF16), w_ref[...], preferred_element_type=F32)

    def three(j):
        gsend[j] = share(j).astype(BF16)
        copy(gsend.at[j], gpart.at[d], gs.at[j], gr.at[d], (e, j)).start()

    peers(N, d, three)
    total = share(d)
    peers(N, d, lambda j: copy(gsend.at[j], gpart.at[j], gs.at[j], gr.at[j], (e, j)).wait_recv())
    total = lax.fori_loop(
        1, N, lambda k, t: t + gpart[lax.rem(d + k, N)].astype(F32), total
    )
    xsend[...] = total[HC:].astype(BF16)
    cross_grad = copy(xsend, xpart, xs.at[1], xr.at[1], (other, d))
    cross_grad.start()
    own_act = jnp.concatenate([act[0, d].astype(F32), act[1, d].astype(F32)], axis=0)
    pg_col = jnp.sum(total * own_act, axis=1, keepdims=True)
    eye = lax.broadcasted_iota(jnp.int32, (EC, EC), 0) == lax.broadcasted_iota(jnp.int32, (EC, EC), 1)
    pg_row = jnp.sum(jnp.where(eye, pg_col, 0.0), axis=0, keepdims=True)
    pg[x] = jnp.broadcast_to(pg_row, (8, EC))
    peers(H, x, lambda j: copy(pg.at[x], pg.at[x], qs.at[j], qr.at[x], (start + j, d)).start())

    def finish(g, grad):
        gate = hid_ref[half_rows(g), :ff].astype(F32)
        up = hid_ref[half_rows(g), ff:].astype(F32)
        sig = jax.nn.sigmoid(gate)
        hidden_ref[half_rows(g), :ff] = (grad * up * sig * (1.0 + gate * (1.0 - sig))).astype(BF16)
        hidden_ref[half_rows(g), ff:] = (grad * gate * sig).astype(BF16)

    finish(mine, total[:HC])

    peers(H, x, lambda j: copy(pg.at[x], pg.at[j], qs.at[j], qr.at[j], (start + j, d)).wait_recv())
    upper = jnp.where(slot >= H, 1, 0)
    away = jnp.where(upper == mine, 0, 1)
    expert = slot - upper * H
    place = position + (away * HC + x * C).astype(F32)
    found = lax.broadcasted_iota(jnp.int32, (tok, EC), 1).astype(F32) == place
    probs_ref[...] = (
        lax.fori_loop(
            0,
            H,
            lambda j, t: t
            + jnp.sum(jnp.where(found & (expert == j), pg[j][0:1, :], 0.0), axis=1, keepdims=True),
            jnp.zeros((tok, 1), F32),
        )
        / prob
    )
    cross_grad.wait_recv()
    finish(1 - mine, xpart[...].astype(F32))

    for c in range(parts):
        copy(psend.at[c], ppart.at[c], ps.at[c], pr.at[c], (other, d)).wait_recv()
        down_ref[c * step : (c + 1) * step, :] += ppart[c].astype(F32)

    def sent_dp(j):
        copy(send1.at[j], got1.at[d], s1s.at[j], s1r.at[d], (e, j)).wait_send()
        for i in range(2):
            copy(act.at[i, d], act.at[i, d], as_.at[i, j], ar.at[i, d], (e, j)).wait_send()
        copy(gsend.at[j], gpart.at[d], gs.at[j], gr.at[d], (e, j)).wait_send()

    def sent_e(j):
        copy(send2.at[j], rows.at[x], s2s.at[j], s2r.at[x], (start + j, d)).wait_send()
        copy(pg.at[x], pg.at[x], qs.at[j], qr.at[x], (start + j, d)).wait_send()

    peers(N, d, sent_dp)
    peers(H, x, sent_e)
    cross_act.wait_send()
    cross_grad.wait_send()
    for c in range(parts):
        copy(psend.at[c], ppart.at[c], ps.at[c], pr.at[c], (other, d)).wait_send()


def on_device(E, N, cotangent, router_probs, slot_ids, saved_hidden, down_weight):
    tok, width = cotangent.shape
    C = 3 * tok // (2 * E)
    H = E // 2
    NC, EC, HC = N * C, E * C, H * C
    block, ff = down_weight.shape[1:]
    parts = max(1, block // 256)
    by_dp = np.array([[j // C * EC + j % C] for j in range(NC)], np.int32)
    by_act = np.array([[j // C * HC + j % C] for j in range(NC)], np.int32)
    by_e = np.array(
        [[i // C % H * 2 * NC + i // HC * NC + i % C] for i in range(EC)], np.int32
    )
    dma = pltpu.SemaphoreType.DMA
    vmem = pl.BlockSpec(memory_space=pltpu.VMEM)
    down, hidden, probs = pl.pallas_call(
        functools.partial(kernel, E, N, C),
        out_shape=(
            jax.ShapeDtypeStruct((block, ff), F32),
            jax.ShapeDtypeStruct((EC, 2 * ff), BF16),
            jax.ShapeDtypeStruct((tok, 1), F32),
        ),
        in_specs=[vmem] * 8,
        out_specs=(vmem,) * 3,
        scratch_shapes=[
            pltpu.VMEM((N, EC, block), BF16),
            pltpu.VMEM((N, EC, block), BF16),
            pltpu.VMEM((2, N, HC, ff), BF16),
            pltpu.VMEM((H, 2, NC, ff), BF16),
            pltpu.VMEM((H, 2, NC, block), BF16),
            pltpu.VMEM((H, 2, NC, block), BF16),
            pltpu.VMEM((N, EC, ff), BF16),
            pltpu.VMEM((N, EC, ff), BF16),
            pltpu.VMEM((parts, block // parts, ff), BF16),
            pltpu.VMEM((parts, block // parts, ff), BF16),
            pltpu.VMEM((H, 8, EC), F32),
            pltpu.VMEM((tok, width), BF16),
            pltpu.VMEM((EC, tok), BF16),
            pltpu.VMEM((HC, ff), BF16),
            pltpu.VMEM((HC, ff), BF16),
            pltpu.VMEM((HC, ff), BF16),
            dma((N,)), dma((N,)), dma((2, N)), dma((2, N)), dma((H,)), dma((H,)),
            dma((N,)), dma((N,)), dma((parts,)), dma((parts,)), dma((H,)), dma((H,)),
            dma((2,)), dma((2,)),
        ],
        compiler_params=pltpu.CompilerParams(
            collective_id=0, has_side_effects=True, vmem_limit_bytes=56 * 2**20
        ),
        name="expert_backward",
    )(cotangent, router_probs, slot_ids, saved_hidden[0], down_weight[0], by_dp, by_act, by_e)
    return down[None], hidden[None], probs


def solution(mesh):
    placed = (
        P(("expert", "dp"), None),
        P(("expert", "dp"), None),
        P(("expert", "dp"), None),
        P("expert", "dp", None),
        P("expert", "dp", None),
    )
    return jax.shard_map(
        functools.partial(on_device, mesh.shape["expert"], mesh.shape["dp"]),
        mesh=mesh,
        in_specs=placed,
        out_specs=(P("expert", "dp", None), P("expert", "dp", None), P(("expert", "dp"), None)),
        check_vma=False,
    )
```

```python
import functools

import jax
import jax.numpy as jnp
import numpy as np
from jax import lax
from jax.experimental import pallas as pl
from jax.experimental.pallas import tpu as pltpu
from jax.sharding import PartitionSpec as P

MESH = pl.DeviceIdType.MESH
F32 = jnp.float32
BF16 = jnp.bfloat16


def kernel(
    E, N, C, cot_ref, prob_ref, slot_ref, hid_ref, w_ref, by_dp_ref, by_act_ref, by_e_ref,
    down_ref, hidden_ref, probs_ref,
    send1, got1, act, act_rows, send2, rows, gsend, gpart, psend, ppart, pg, scaled, spread,
    xact, xsend, xpart, s1s, s1r, as_, ar, s2s, s2r, gs, gr, ps, pr, qs, qr, xs, xr,
):
    e, d = lax.axis_index("expert"), lax.axis_index("dp")
    tok, width = cot_ref.shape
    block = width // N
    ff = act.shape[3]
    H = E // 2
    NC, EC, HC = N * C, E * C, H * C
    mine, x = lax.div(e, H), lax.rem(e, H)
    other = lax.rem(e + H, E)
    start = mine * H

    def copy(src, dst, ss, rs, where):
        return pltpu.make_async_remote_copy(
            src_ref=src, dst_ref=dst, send_sem=ss, recv_sem=rs, device_id=where, device_id_type=MESH
        )

    def peers(n, me, body):
        def step(k, carry):
            body(lax.rem(me + k, n))
            return carry

        lax.fori_loop(1, n, step, 0)

    barrier = pltpu.get_barrier_semaphore()
    peers(N, d, lambda j: pl.semaphore_signal(barrier, inc=1, device_id=(e, j), device_id_type=MESH))
    peers(
        H, x,
        lambda j: pl.semaphore_signal(barrier, inc=1, device_id=(start + j, d), device_id_type=MESH),
    )
    pl.semaphore_signal(barrier, inc=1, device_id=(other, d), device_id_type=MESH)

    def half_rows(g):
        return pl.ds(pl.multiple_of(g * HC, HC), HC)

    def activation(g):
        gate = hid_ref[half_rows(g), :ff].astype(F32)
        up = hid_ref[half_rows(g), ff:].astype(F32)
        return (gate * jax.nn.sigmoid(gate) * up).astype(BF16)

    xact[...] = activation(1 - mine)

    slot = slot_ref[...]
    lanes = lax.broadcasted_iota(jnp.int32, (tok, 128), 1)
    hits = jnp.where(lanes == slot, 1.0, 0.0).astype(F32)
    row_i = lax.broadcasted_iota(jnp.int32, (tok, tok), 0)
    col_i = lax.broadcasted_iota(jnp.int32, (tok, tok), 1)
    before = jnp.where(col_i < row_i, 1.0, 0.0).astype(BF16)
    earlier = jnp.dot(before, hits.astype(BF16), preferred_element_type=F32)
    position = jnp.sum(earlier * hits, axis=1, keepdims=True)
    target = slot.astype(F32) * C + position
    target_row = jnp.sum(jnp.where(row_i == col_i, target, 0.0), axis=0, keepdims=True)
    spread[...] = jnp.where(
        lax.broadcasted_iota(jnp.int32, (EC, tok), 0).astype(F32) == target_row, 1.0, 0.0
    ).astype(BF16)
    prob = prob_ref[...].astype(F32)
    scaled[...] = (cot_ref[...].astype(F32) * prob).astype(BF16)

    parts = psend.shape[0]
    step = block // parts

    def piece(j, c):
        cols = pl.ds(pl.multiple_of(j * block + c * step, step), step)
        return jnp.dot(spread[...], scaled[:, cols], preferred_element_type=F32).astype(BF16)

    pl.semaphore_wait(barrier, N - 1 + H)
    cross_act = copy(xact, act.at[1, d], xs.at[0], xr.at[0], (other, d))
    cross_act.start()

    for c in range(parts):

        def one(j):
            send1[c, j] = piece(j, c)
            copy(send1.at[c, j], got1.at[c, d], s1s.at[c, j], s1r.at[c, d], (e, j)).start()

        peers(N, d, one)
        got1[c, d] = piece(d, c)

    act[0, d] = activation(mine)

    def give(i):
        peers(N, d, lambda j: copy(act.at[i, d], act.at[i, d], as_.at[i, j], ar.at[i, d], (e, j)).start())

    give(0)
    lane_r = lax.broadcasted_iota(jnp.int32, (NC, N * EC), 1)

    def select(base, ref):
        pick = jnp.where(lane_r == base, 1.0, 0.0).astype(BF16)
        return jnp.dot(pick, ref.reshape(N * EC, ref.shape[-1]), preferred_element_type=F32).astype(BF16)

    def rows_of(s, c):
        return select(by_dp_ref[...] + s * C, got1[c])

    for c in range(parts):
        peers(
            N, d,
            lambda j: copy(
                send1.at[c, j], got1.at[c, j], s1s.at[c, j], s1r.at[c, j], (e, j)
            ).wait_recv(),
        )

        def two(j):
            send2[c, j, 0] = rows_of(start + j, c)
            send2[c, j, 1] = rows_of((1 - mine) * H + j, c)
            copy(
                send2.at[c, j], rows.at[c, x], s2s.at[c, j], s2r.at[c, x], (start + j, d)
            ).start()

        peers(H, x, two)
        rows[c, x, 0] = rows_of(e, c)
        rows[c, x, 1] = rows_of(other, c)
        if c == 0:
            cross_act.wait_recv()
            give(1)

    for i in range(2):
        peers(
            N, d,
            lambda j: copy(act.at[i, d], act.at[i, j], as_.at[i, j], ar.at[i, j], (e, j)).wait_recv(),
        )

    def order(j, carry):
        for i in range(2):
            act_rows[j, i] = select(by_act_ref[...] + (i * N * HC + j * C), act[...])
        return carry

    lax.fori_loop(0, H, order, 0)
    lined = act_rows[...].reshape(E * NC, ff)
    for c in range(parts):
        peers(
            H, x,
            lambda j: copy(
                send2.at[c, j], rows.at[c, j], s2s.at[c, j], s2r.at[c, j], (start + j, d)
            ).wait_recv(),
        )
        left = rows[c].reshape(E * NC, step)
        grad = lax.dot_general(left, lined, (((0,), (0,)), ((), ())), preferred_element_type=F32)
        down_ref[c * step : (c + 1) * step, :] = grad
        psend[c] = grad.astype(BF16)
        copy(psend.at[c], ppart.at[c], ps.at[c], pr.at[c], (other, d)).start()

    lane_g = lax.broadcasted_iota(jnp.int32, (EC, E * NC), 1)

    def share(j):
        pick = jnp.where(lane_g == by_e_ref[...] + j * C, 1.0, 0.0).astype(BF16)
        part = jnp.zeros((EC, ff), F32)
        for c in range(parts):
            ordered = jnp.dot(pick, rows[c].reshape(E * NC, step), preferred_element_type=F32)
            part += jnp.dot(
                ordered.astype(BF16), w_ref[c * step : (c + 1) * step, :], preferred_element_type=F32
            )
        return part

    def three(j):
        gsend[j] = share(j).astype(BF16)
        copy(gsend.at[j], gpart.at[d], gs.at[j], gr.at[d], (e, j)).start()

    peers(N, d, three)
    total = share(d)
    peers(N, d, lambda j: copy(gsend.at[j], gpart.at[j], gs.at[j], gr.at[j], (e, j)).wait_recv())
    total = lax.fori_loop(
        1, N, lambda k, t: t + gpart[lax.rem(d + k, N)].astype(F32), total
    )
    xsend[...] = total[HC:].astype(BF16)
    cross_grad = copy(xsend, xpart, xs.at[1], xr.at[1], (other, d))
    cross_grad.start()
    own_act = jnp.concatenate([act[0, d].astype(F32), act[1, d].astype(F32)], axis=0)
    pg_col = jnp.sum(total * own_act, axis=1, keepdims=True)
    eye = lax.broadcasted_iota(jnp.int32, (EC, EC), 0) == lax.broadcasted_iota(jnp.int32, (EC, EC), 1)
    pg_row = jnp.sum(jnp.where(eye, pg_col, 0.0), axis=0, keepdims=True)
    pg[x] = jnp.broadcast_to(pg_row, (8, EC))
    peers(H, x, lambda j: copy(pg.at[x], pg.at[x], qs.at[j], qr.at[x], (start + j, d)).start())

    def finish(g, grad):
        gate = hid_ref[half_rows(g), :ff].astype(F32)
        up = hid_ref[half_rows(g), ff:].astype(F32)
        sig = jax.nn.sigmoid(gate)
        hidden_ref[half_rows(g), :ff] = (grad * up * sig * (1.0 + gate * (1.0 - sig))).astype(BF16)
        hidden_ref[half_rows(g), ff:] = (grad * gate * sig).astype(BF16)

    finish(mine, total[:HC])

    peers(H, x, lambda j: copy(pg.at[x], pg.at[j], qs.at[j], qr.at[j], (start + j, d)).wait_recv())
    upper = jnp.where(slot >= H, 1, 0)
    away = jnp.where(upper == mine, 0, 1)
    expert = slot - upper * H
    place = position + (away * HC + x * C).astype(F32)
    found = lax.broadcasted_iota(jnp.int32, (tok, EC), 1).astype(F32) == place
    probs_ref[...] = (
        lax.fori_loop(
            0,
            H,
            lambda j, t: t
            + jnp.sum(jnp.where(found & (expert == j), pg[j][0:1, :], 0.0), axis=1, keepdims=True),
            jnp.zeros((tok, 1), F32),
        )
        / prob
    )
    cross_grad.wait_recv()
    finish(1 - mine, xpart[...].astype(F32))

    for c in range(parts):
        copy(psend.at[c], ppart.at[c], ps.at[c], pr.at[c], (other, d)).wait_recv()
        down_ref[c * step : (c + 1) * step, :] += ppart[c].astype(F32)

    def sent_dp(j):
        for c in range(parts):
            copy(send1.at[c, j], got1.at[c, d], s1s.at[c, j], s1r.at[c, d], (e, j)).wait_send()
        for i in range(2):
            copy(act.at[i, d], act.at[i, d], as_.at[i, j], ar.at[i, d], (e, j)).wait_send()
        copy(gsend.at[j], gpart.at[d], gs.at[j], gr.at[d], (e, j)).wait_send()

    def sent_e(j):
        for c in range(parts):
            copy(
                send2.at[c, j], rows.at[c, x], s2s.at[c, j], s2r.at[c, x], (start + j, d)
            ).wait_send()
        copy(pg.at[x], pg.at[x], qs.at[j], qr.at[x], (start + j, d)).wait_send()

    peers(N, d, sent_dp)
    peers(H, x, sent_e)
    cross_act.wait_send()
    cross_grad.wait_send()
    for c in range(parts):
        copy(psend.at[c], ppart.at[c], ps.at[c], pr.at[c], (other, d)).wait_send()


def on_device(E, N, cotangent, router_probs, slot_ids, saved_hidden, down_weight):
    tok, width = cotangent.shape
    C = 3 * tok // (2 * E)
    H = E // 2
    NC, EC, HC = N * C, E * C, H * C
    block, ff = down_weight.shape[1:]
    parts = max(1, block // 256)
    by_dp = np.array([[j // C * EC + j % C] for j in range(NC)], np.int32)
    by_act = np.array([[j // C * HC + j % C] for j in range(NC)], np.int32)
    by_e = np.array(
        [[i // C % H * 2 * NC + i // HC * NC + i % C] for i in range(EC)], np.int32
    )
    dma = pltpu.SemaphoreType.DMA
    vmem = pl.BlockSpec(memory_space=pltpu.VMEM)
    down, hidden, probs = pl.pallas_call(
        functools.partial(kernel, E, N, C),
        out_shape=(
            jax.ShapeDtypeStruct((block, ff), F32),
            jax.ShapeDtypeStruct((EC, 2 * ff), BF16),
            jax.ShapeDtypeStruct((tok, 1), F32),
        ),
        in_specs=[vmem] * 8,
        out_specs=(vmem,) * 3,
        scratch_shapes=[
            pltpu.VMEM((parts, N, EC, block // parts), BF16),
            pltpu.VMEM((parts, N, EC, block // parts), BF16),
            pltpu.VMEM((2, N, HC, ff), BF16),
            pltpu.VMEM((H, 2, NC, ff), BF16),
            pltpu.VMEM((parts, H, 2, NC, block // parts), BF16),
            pltpu.VMEM((parts, H, 2, NC, block // parts), BF16),
            pltpu.VMEM((N, EC, ff), BF16),
            pltpu.VMEM((N, EC, ff), BF16),
            pltpu.VMEM((parts, block // parts, ff), BF16),
            pltpu.VMEM((parts, block // parts, ff), BF16),
            pltpu.VMEM((H, 8, EC), F32),
            pltpu.VMEM((tok, width), BF16),
            pltpu.VMEM((EC, tok), BF16),
            pltpu.VMEM((HC, ff), BF16),
            pltpu.VMEM((HC, ff), BF16),
            pltpu.VMEM((HC, ff), BF16),
            dma((parts, N)), dma((parts, N)), dma((2, N)), dma((2, N)), dma((parts, H)), dma((parts, H)),
            dma((N,)), dma((N,)), dma((parts,)), dma((parts,)), dma((H,)), dma((H,)),
            dma((2,)), dma((2,)),
        ],
        compiler_params=pltpu.CompilerParams(
            collective_id=0, has_side_effects=True, vmem_limit_bytes=56 * 2**20
        ),
        name="expert_backward",
    )(cotangent, router_probs, slot_ids, saved_hidden[0], down_weight[0], by_dp, by_act, by_e)
    return down[None], hidden[None], probs


def solution(mesh):
    placed = (
        P(("expert", "dp"), None),
        P(("expert", "dp"), None),
        P(("expert", "dp"), None),
        P("expert", "dp", None),
        P("expert", "dp", None),
    )
    return jax.shard_map(
        functools.partial(on_device, mesh.shape["expert"], mesh.shape["dp"]),
        mesh=mesh,
        in_specs=placed,
        out_specs=(P("expert", "dp", None), P("expert", "dp", None), P(("expert", "dp"), None)),
        check_vma=False,
    )
```

```python
import functools

import jax
import jax.numpy as jnp
import numpy as np
from jax import lax
from jax.experimental import pallas as pl
from jax.experimental.pallas import tpu as pltpu
from jax.sharding import PartitionSpec as P

MESH = pl.DeviceIdType.MESH
F32 = jnp.float32
BF16 = jnp.bfloat16


def kernel(
    E, N, C, cot_ref, prob_ref, slot_ref, hid_ref, w_ref, by_dp_ref, by_act_ref, by_e_ref,
    down_ref, hidden_ref, probs_ref,
    send1, got1, act, act_rows, send2, rows, gsend, gpart, psend, ppart, pg, scaled, spread,
    xact, xsend, xpart, s1s, s1r, as_, ar, s2s, s2r, gs, gr, ps, pr, qs, qr, xs, xr,
):
    e, d = lax.axis_index("expert"), lax.axis_index("dp")
    tok, width = cot_ref.shape
    block = width // N
    ff = act.shape[3]
    H = E // 2
    NC, EC, HC = N * C, E * C, H * C
    mine, x = lax.div(e, H), lax.rem(e, H)
    other = lax.rem(e + H, E)
    start = mine * H

    def copy(src, dst, ss, rs, where):
        return pltpu.make_async_remote_copy(
            src_ref=src, dst_ref=dst, send_sem=ss, recv_sem=rs, device_id=where, device_id_type=MESH
        )

    def peers(n, me, body):
        def step(k, carry):
            body(lax.rem(me + k, n))
            return carry

        lax.fori_loop(1, n, step, 0, unroll=n <= 8)

    barrier = pltpu.get_barrier_semaphore()
    peers(N, d, lambda j: pl.semaphore_signal(barrier, inc=1, device_id=(e, j), device_id_type=MESH))
    peers(
        H, x,
        lambda j: pl.semaphore_signal(barrier, inc=1, device_id=(start + j, d), device_id_type=MESH),
    )
    pl.semaphore_signal(barrier, inc=1, device_id=(other, d), device_id_type=MESH)

    def half_rows(g):
        return pl.ds(pl.multiple_of(g * HC, HC), HC)

    def activation(g):
        gate = hid_ref[half_rows(g), :ff].astype(F32)
        up = hid_ref[half_rows(g), ff:].astype(F32)
        return (gate * jax.nn.sigmoid(gate) * up).astype(BF16)

    xact[...] = activation(1 - mine)

    slot = slot_ref[...]
    lanes = lax.broadcasted_iota(jnp.int32, (tok, 128), 1)
    hits = jnp.where(lanes == slot, 1.0, 0.0).astype(F32)
    row_i = lax.broadcasted_iota(jnp.int32, (tok, tok), 0)
    col_i = lax.broadcasted_iota(jnp.int32, (tok, tok), 1)
    before = jnp.where(col_i < row_i, 1.0, 0.0).astype(BF16)
    earlier = jnp.dot(before, hits.astype(BF16), preferred_element_type=F32)
    position = jnp.sum(earlier * hits, axis=1, keepdims=True)
    target = slot.astype(F32) * C + position
    target_row = jnp.sum(jnp.where(row_i == col_i, target, 0.0), axis=0, keepdims=True)
    spread[...] = jnp.where(
        lax.broadcasted_iota(jnp.int32, (EC, tok), 0).astype(F32) == target_row, 1.0, 0.0
    ).astype(BF16)
    prob = prob_ref[...].astype(F32)
    scaled[...] = (cot_ref[...].astype(F32) * prob).astype(BF16)

    def piece(j):
        cols = pl.ds(pl.multiple_of(j * block, block), block)
        return jnp.dot(spread[...], scaled[:, cols], preferred_element_type=F32).astype(BF16)

    pl.semaphore_wait(barrier, N - 1 + H)
    cross_act = copy(xact, act.at[1, d], xs.at[0], xr.at[0], (other, d))
    cross_act.start()

    def one(j):
        send1[j] = piece(j)
        copy(send1.at[j], got1.at[d], s1s.at[j], s1r.at[d], (e, j)).start()

    peers(N, d, one)
    got1[d] = piece(d)

    act[0, d] = activation(mine)

    def give(i):
        peers(N, d, lambda j: copy(act.at[i, d], act.at[i, d], as_.at[i, j], ar.at[i, d], (e, j)).start())

    give(0)
    peers(N, d, lambda j: copy(send1.at[j], got1.at[j], s1s.at[j], s1r.at[j], (e, j)).wait_recv())

    lane_r = lax.broadcasted_iota(jnp.int32, (2 * NC, N * EC), 1)
    second = lax.broadcasted_iota(jnp.int32, (2 * NC, 1), 0) >= NC

    def select(base, ref):
        pick = jnp.where(lane_r == base, 1.0, 0.0).astype(BF16)
        whole = ref[...].reshape(N * EC, ref.shape[-1])
        picked = jnp.dot(pick, whole, preferred_element_type=F32).astype(BF16)
        return picked.reshape(2, NC, ref.shape[-1])

    def rows_of(j):
        first = (start + j) * C
        return select(by_dp_ref[...] + jnp.where(second, ((1 - mine) * H + j) * C, first), got1)

    def two(j):
        send2[j] = rows_of(j)
        copy(send2.at[j], rows.at[x], s2s.at[j], s2r.at[x], (start + j, d)).start()

    peers(H, x, two)
    cross_act.wait_recv()
    give(1)
    rows[x] = rows_of(x)

    for i in range(2):
        peers(
            N, d,
            lambda j: copy(act.at[i, d], act.at[i, j], as_.at[i, j], ar.at[i, j], (e, j)).wait_recv(),
        )

    def order(j, carry):
        act_rows[j] = select(by_act_ref[...] + j * C, act)
        return carry

    lax.fori_loop(0, H, order, 0, unroll=H <= 8)
    peers(
        H, x,
        lambda j: copy(send2.at[j], rows.at[j], s2s.at[j], s2r.at[j], (start + j, d)).wait_recv(),
    )

    parts = psend.shape[0]
    step = block // parts
    lined = act_rows[...].reshape(E * NC, ff)
    for c in range(parts):
        left = rows[:, :, :, c * step : (c + 1) * step].reshape(E * NC, step)
        grad = lax.dot_general(left, lined, (((0,), (0,)), ((), ())), preferred_element_type=F32)
        down_ref[c * step : (c + 1) * step, :] = grad
        psend[c] = grad.astype(BF16)
        copy(psend.at[c], ppart.at[c], ps.at[c], pr.at[c], (other, d)).start()

    lane_g = lax.broadcasted_iota(jnp.int32, (EC, E * NC), 1)

    def share(j):
        pick = jnp.where(lane_g == by_e_ref[...] + j * C, 1.0, 0.0).astype(BF16)
        ordered = jnp.dot(pick, rows[...].reshape(E * NC, block), preferred_element_type=F32)
        return jnp.dot(ordered.astype(BF16), w_ref[...], preferred_element_type=F32)

    def three(j):
        gsend[j] = share(j).astype(BF16)
        copy(gsend.at[j], gpart.at[d], gs.at[j], gr.at[d], (e, j)).start()

    peers(N, d, three)
    total = share(d)
    peers(N, d, lambda j: copy(gsend.at[j], gpart.at[j], gs.at[j], gr.at[j], (e, j)).wait_recv())
    total = lax.fori_loop(
        1, N, lambda k, t: t + gpart[lax.rem(d + k, N)].astype(F32), total
    )
    xsend[...] = total[HC:].astype(BF16)
    cross_grad = copy(xsend, xpart, xs.at[1], xr.at[1], (other, d))
    cross_grad.start()
    own_act = jnp.concatenate([act[0, d].astype(F32), act[1, d].astype(F32)], axis=0)
    pg_col = jnp.sum(total * own_act, axis=1, keepdims=True)
    eye = lax.broadcasted_iota(jnp.int32, (EC, EC), 0) == lax.broadcasted_iota(jnp.int32, (EC, EC), 1)
    pg_row = jnp.sum(jnp.where(eye, pg_col, 0.0), axis=0, keepdims=True)
    pg[x] = jnp.broadcast_to(pg_row, (8, EC))
    peers(H, x, lambda j: copy(pg.at[x], pg.at[x], qs.at[j], qr.at[x], (start + j, d)).start())

    def finish(g, grad):
        gate = hid_ref[half_rows(g), :ff].astype(F32)
        up = hid_ref[half_rows(g), ff:].astype(F32)
        sig = jax.nn.sigmoid(gate)
        hidden_ref[half_rows(g), :ff] = (grad * up * sig * (1.0 + gate * (1.0 - sig))).astype(BF16)
        hidden_ref[half_rows(g), ff:] = (grad * gate * sig).astype(BF16)

    finish(mine, total[:HC])

    peers(H, x, lambda j: copy(pg.at[x], pg.at[j], qs.at[j], qr.at[j], (start + j, d)).wait_recv())
    upper = jnp.where(slot >= H, 1, 0)
    away = jnp.where(upper == mine, 0, 1)
    expert = slot - upper * H
    place = position + (away * HC + x * C).astype(F32)
    found = lax.broadcasted_iota(jnp.int32, (tok, EC), 1).astype(F32) == place
    probs_ref[...] = (
        lax.fori_loop(
            0,
            H,
            lambda j, t: t
            + jnp.sum(jnp.where(found & (expert == j), pg[j][0:1, :], 0.0), axis=1, keepdims=True),
            jnp.zeros((tok, 1), F32),
        )
        / prob
    )
    cross_grad.wait_recv()
    finish(1 - mine, xpart[...].astype(F32))

    for c in range(parts):
        copy(psend.at[c], ppart.at[c], ps.at[c], pr.at[c], (other, d)).wait_recv()
        down_ref[c * step : (c + 1) * step, :] += ppart[c].astype(F32)

    def sent_dp(j):
        copy(send1.at[j], got1.at[d], s1s.at[j], s1r.at[d], (e, j)).wait_send()
        for i in range(2):
            copy(act.at[i, d], act.at[i, d], as_.at[i, j], ar.at[i, d], (e, j)).wait_send()
        copy(gsend.at[j], gpart.at[d], gs.at[j], gr.at[d], (e, j)).wait_send()

    def sent_e(j):
        copy(send2.at[j], rows.at[x], s2s.at[j], s2r.at[x], (start + j, d)).wait_send()
        copy(pg.at[x], pg.at[x], qs.at[j], qr.at[x], (start + j, d)).wait_send()

    peers(N, d, sent_dp)
    peers(H, x, sent_e)
    cross_act.wait_send()
    cross_grad.wait_send()
    for c in range(parts):
        copy(psend.at[c], ppart.at[c], ps.at[c], pr.at[c], (other, d)).wait_send()


def on_device(E, N, cotangent, router_probs, slot_ids, saved_hidden, down_weight):
    tok, width = cotangent.shape
    C = 3 * tok // (2 * E)
    H = E // 2
    NC, EC, HC = N * C, E * C, H * C
    block, ff = down_weight.shape[1:]
    parts = max(1, block // 256)
    by_dp = np.array([[j // C * EC + j % C] for j in range(NC)] * 2, np.int32)
    by_act = np.array([[i * N * HC + j // C * HC + j % C] for i in range(2) for j in range(NC)], np.int32)
    by_e = np.array(
        [[i // C % H * 2 * NC + i // HC * NC + i % C] for i in range(EC)], np.int32
    )
    dma = pltpu.SemaphoreType.DMA
    vmem = pl.BlockSpec(memory_space=pltpu.VMEM)
    down, hidden, probs = pl.pallas_call(
        functools.partial(kernel, E, N, C),
        out_shape=(
            jax.ShapeDtypeStruct((block, ff), F32),
            jax.ShapeDtypeStruct((EC, 2 * ff), BF16),
            jax.ShapeDtypeStruct((tok, 1), F32),
        ),
        in_specs=[vmem] * 8,
        out_specs=(vmem,) * 3,
        scratch_shapes=[
            pltpu.VMEM((N, EC, block), BF16),
            pltpu.VMEM((N, EC, block), BF16),
            pltpu.VMEM((2, N, HC, ff), BF16),
            pltpu.VMEM((H, 2, NC, ff), BF16),
            pltpu.VMEM((H, 2, NC, block), BF16),
            pltpu.VMEM((H, 2, NC, block), BF16),
            pltpu.VMEM((N, EC, ff), BF16),
            pltpu.VMEM((N, EC, ff), BF16),
            pltpu.VMEM((parts, block // parts, ff), BF16),
            pltpu.VMEM((parts, block // parts, ff), BF16),
            pltpu.VMEM((H, 8, EC), F32),
            pltpu.VMEM((tok, width), BF16),
            pltpu.VMEM((EC, tok), BF16),
            pltpu.VMEM((HC, ff), BF16),
            pltpu.VMEM((HC, ff), BF16),
            pltpu.VMEM((HC, ff), BF16),
            dma((N,)), dma((N,)), dma((2, N)), dma((2, N)), dma((H,)), dma((H,)),
            dma((N,)), dma((N,)), dma((parts,)), dma((parts,)), dma((H,)), dma((H,)),
            dma((2,)), dma((2,)),
        ],
        compiler_params=pltpu.CompilerParams(
            collective_id=0, has_side_effects=True, vmem_limit_bytes=56 * 2**20
        ),
        name="expert_backward",
    )(cotangent, router_probs, slot_ids, saved_hidden[0], down_weight[0], by_dp, by_act, by_e)
    return down[None], hidden[None], probs


def solution(mesh):
    placed = (
        P(("expert", "dp"), None),
        P(("expert", "dp"), None),
        P(("expert", "dp"), None),
        P("expert", "dp", None),
        P("expert", "dp", None),
    )
    return jax.shard_map(
        functools.partial(on_device, mesh.shape["expert"], mesh.shape["dp"]),
        mesh=mesh,
        in_specs=placed,
        out_specs=(P("expert", "dp", None), P("expert", "dp", None), P(("expert", "dp"), None)),
        check_vma=False,
    )
```

```python
import functools

import jax
import jax.numpy as jnp
import numpy as np
from jax import lax
from jax.experimental import pallas as pl
from jax.experimental.pallas import tpu as pltpu
from jax.sharding import PartitionSpec as P

MESH = pl.DeviceIdType.MESH
F32 = jnp.float32
BF16 = jnp.bfloat16


def kernel(
    E, N, C, cot_ref, prob_ref, slot_ref, hid_ref, w_ref, by_dp_ref, by_act_ref, by_e_ref,
    down_ref, hidden_ref, probs_ref,
    send1, got1, act, act_rows, send2, rows, gsend, gpart, psend, ppart, pg, scaled, spread,
    xact, xsend, xpart, s1s, s1r, as_, ar, s2s, s2r, gs, gr, ps, pr, qs, qr, xs, xr,
):
    e, d = lax.axis_index("expert"), lax.axis_index("dp")
    tok, width = cot_ref.shape
    block = width // N
    ff = act.shape[3]
    H = E // 2
    NC, EC, HC = N * C, E * C, H * C
    mine, x = lax.div(e, H), lax.rem(e, H)
    other = lax.rem(e + H, E)
    start = mine * H

    def copy(src, dst, ss, rs, where):
        return pltpu.make_async_remote_copy(
            src_ref=src, dst_ref=dst, send_sem=ss, recv_sem=rs, device_id=where, device_id_type=MESH
        )

    def peers(n, me, body):
        def step(k, carry):
            body(lax.rem(me + k, n))
            return carry

        lax.fori_loop(1, n, step, 0, unroll=n <= 8)

    barrier = pltpu.get_barrier_semaphore()
    peers(N, d, lambda j: pl.semaphore_signal(barrier, inc=1, device_id=(e, j), device_id_type=MESH))
    peers(
        H, x,
        lambda j: pl.semaphore_signal(barrier, inc=1, device_id=(start + j, d), device_id_type=MESH),
    )
    pl.semaphore_signal(barrier, inc=1, device_id=(other, d), device_id_type=MESH)

    def half_rows(g):
        return pl.ds(pl.multiple_of(g * HC, HC), HC)

    def activation(g):
        gate = hid_ref[half_rows(g), :ff].astype(F32)
        up = hid_ref[half_rows(g), ff:].astype(F32)
        return (gate * jax.nn.sigmoid(gate) * up).astype(BF16)

    xact[...] = activation(1 - mine)

    slot = slot_ref[...]
    lanes = lax.broadcasted_iota(jnp.int32, (tok, 128), 1)
    hits = jnp.where(lanes == slot, 1.0, 0.0).astype(F32)
    row_i = lax.broadcasted_iota(jnp.int32, (tok, tok), 0)
    col_i = lax.broadcasted_iota(jnp.int32, (tok, tok), 1)
    before = jnp.where(col_i < row_i, 1.0, 0.0).astype(BF16)
    earlier = jnp.dot(before, hits.astype(BF16), preferred_element_type=F32)
    position = jnp.sum(earlier * hits, axis=1, keepdims=True)
    target = slot.astype(F32) * C + position
    target_row = jnp.sum(jnp.where(row_i == col_i, target, 0.0), axis=0, keepdims=True)
    spread[...] = jnp.where(
        lax.broadcasted_iota(jnp.int32, (EC, tok), 0).astype(F32) == target_row, 1.0, 0.0
    ).astype(BF16)
    prob = prob_ref[...].astype(F32)
    scaled[...] = (cot_ref[...].astype(F32) * prob).astype(BF16)

    parts = psend.shape[0]
    step = block // parts

    def piece(j, c):
        cols = pl.ds(pl.multiple_of(j * block + c * step, step), step)
        return jnp.dot(spread[...], scaled[:, cols], preferred_element_type=F32).astype(BF16)

    pl.semaphore_wait(barrier, N - 1 + H)
    cross_act = copy(xact, act.at[1, d], xs.at[0], xr.at[0], (other, d))
    cross_act.start()

    for c in range(parts):

        def one(j):
            send1[c, j] = piece(j, c)
            copy(send1.at[c, j], got1.at[c, d], s1s.at[c, j], s1r.at[c, d], (e, j)).start()

        peers(N, d, one)
        got1[c, d] = piece(d, c)

    act[0, d] = activation(mine)

    def give(i):
        peers(N, d, lambda j: copy(act.at[i, d], act.at[i, d], as_.at[i, j], ar.at[i, d], (e, j)).start())

    give(0)
    lane_r = lax.broadcasted_iota(jnp.int32, (2 * NC, N * EC), 1)
    second = lax.broadcasted_iota(jnp.int32, (2 * NC, 1), 0) >= NC

    def select(base, ref):
        pick = jnp.where(lane_r == base, 1.0, 0.0).astype(BF16)
        picked = jnp.dot(pick, ref.reshape(N * EC, ref.shape[-1]), preferred_element_type=F32).astype(BF16)
        return picked.reshape(2, NC, ref.shape[-1])

    def rows_of(j, c):
        first = (start + j) * C
        return select(by_dp_ref[...] + jnp.where(second, ((1 - mine) * H + j) * C, first), got1[c])

    for c in range(parts):
        peers(
            N, d,
            lambda j: copy(
                send1.at[c, j], got1.at[c, j], s1s.at[c, j], s1r.at[c, j], (e, j)
            ).wait_recv(),
        )

        def two(j):
            send2[c, j] = rows_of(j, c)
            copy(
                send2.at[c, j], rows.at[c, x], s2s.at[c, j], s2r.at[c, x], (start + j, d)
            ).start()

        peers(H, x, two)
        rows[c, x] = rows_of(x, c)
        if c == 0:
            cross_act.wait_recv()
            give(1)

    for i in range(2):
        peers(
            N, d,
            lambda j: copy(act.at[i, d], act.at[i, j], as_.at[i, j], ar.at[i, j], (e, j)).wait_recv(),
        )

    def order(j, carry):
        act_rows[j] = select(by_act_ref[...] + j * C, act[...])
        return carry

    lax.fori_loop(0, H, order, 0, unroll=H <= 8)
    lined = act_rows[...].reshape(E * NC, ff)
    for c in range(parts):
        peers(
            H, x,
            lambda j: copy(
                send2.at[c, j], rows.at[c, j], s2s.at[c, j], s2r.at[c, j], (start + j, d)
            ).wait_recv(),
        )
        left = rows[c].reshape(E * NC, step)
        grad = lax.dot_general(left, lined, (((0,), (0,)), ((), ())), preferred_element_type=F32)
        down_ref[c * step : (c + 1) * step, :] = grad
        psend[c] = grad.astype(BF16)
        copy(psend.at[c], ppart.at[c], ps.at[c], pr.at[c], (other, d)).start()

    lane_g = lax.broadcasted_iota(jnp.int32, (EC, E * NC), 1)

    def share(j):
        pick = jnp.where(lane_g == by_e_ref[...] + j * C, 1.0, 0.0).astype(BF16)
        part = jnp.zeros((EC, ff), F32)
        for c in range(parts):
            ordered = jnp.dot(pick, rows[c].reshape(E * NC, step), preferred_element_type=F32)
            part += jnp.dot(
                ordered.astype(BF16), w_ref[c * step : (c + 1) * step, :], preferred_element_type=F32
            )
        return part

    def three(j):
        gsend[j] = share(j).astype(BF16)
        copy(gsend.at[j], gpart.at[d], gs.at[j], gr.at[d], (e, j)).start()

    peers(N, d, three)
    total = share(d)
    peers(N, d, lambda j: copy(gsend.at[j], gpart.at[j], gs.at[j], gr.at[j], (e, j)).wait_recv())
    total = lax.fori_loop(
        1, N, lambda k, t: t + gpart[lax.rem(d + k, N)].astype(F32), total
    )
    xsend[...] = total[HC:].astype(BF16)
    cross_grad = copy(xsend, xpart, xs.at[1], xr.at[1], (other, d))
    cross_grad.start()
    own_act = jnp.concatenate([act[0, d].astype(F32), act[1, d].astype(F32)], axis=0)
    pg_col = jnp.sum(total * own_act, axis=1, keepdims=True)
    eye = lax.broadcasted_iota(jnp.int32, (EC, EC), 0) == lax.broadcasted_iota(jnp.int32, (EC, EC), 1)
    pg_row = jnp.sum(jnp.where(eye, pg_col, 0.0), axis=0, keepdims=True)
    pg[x] = jnp.broadcast_to(pg_row, (8, EC))
    peers(H, x, lambda j: copy(pg.at[x], pg.at[x], qs.at[j], qr.at[x], (start + j, d)).start())

    def finish(g, grad):
        gate = hid_ref[half_rows(g), :ff].astype(F32)
        up = hid_ref[half_rows(g), ff:].astype(F32)
        sig = jax.nn.sigmoid(gate)
        hidden_ref[half_rows(g), :ff] = (grad * up * sig * (1.0 + gate * (1.0 - sig))).astype(BF16)
        hidden_ref[half_rows(g), ff:] = (grad * gate * sig).astype(BF16)

    finish(mine, total[:HC])

    peers(H, x, lambda j: copy(pg.at[x], pg.at[j], qs.at[j], qr.at[j], (start + j, d)).wait_recv())
    upper = jnp.where(slot >= H, 1, 0)
    away = jnp.where(upper == mine, 0, 1)
    expert = slot - upper * H
    place = position + (away * HC + x * C).astype(F32)
    found = lax.broadcasted_iota(jnp.int32, (tok, EC), 1).astype(F32) == place
    probs_ref[...] = (
        lax.fori_loop(
            0,
            H,
            lambda j, t: t
            + jnp.sum(jnp.where(found & (expert == j), pg[j][0:1, :], 0.0), axis=1, keepdims=True),
            jnp.zeros((tok, 1), F32),
        )
        / prob
    )
    cross_grad.wait_recv()
    finish(1 - mine, xpart[...].astype(F32))

    for c in range(parts):
        copy(psend.at[c], ppart.at[c], ps.at[c], pr.at[c], (other, d)).wait_recv()
        down_ref[c * step : (c + 1) * step, :] += ppart[c].astype(F32)

    def sent_dp(j):
        for c in range(parts):
            copy(send1.at[c, j], got1.at[c, d], s1s.at[c, j], s1r.at[c, d], (e, j)).wait_send()
        for i in range(2):
            copy(act.at[i, d], act.at[i, d], as_.at[i, j], ar.at[i, d], (e, j)).wait_send()
        copy(gsend.at[j], gpart.at[d], gs.at[j], gr.at[d], (e, j)).wait_send()

    def sent_e(j):
        for c in range(parts):
            copy(
                send2.at[c, j], rows.at[c, x], s2s.at[c, j], s2r.at[c, x], (start + j, d)
            ).wait_send()
        copy(pg.at[x], pg.at[x], qs.at[j], qr.at[x], (start + j, d)).wait_send()

    peers(N, d, sent_dp)
    peers(H, x, sent_e)
    cross_act.wait_send()
    cross_grad.wait_send()
    for c in range(parts):
        copy(psend.at[c], ppart.at[c], ps.at[c], pr.at[c], (other, d)).wait_send()


def on_device(E, N, cotangent, router_probs, slot_ids, saved_hidden, down_weight):
    tok, width = cotangent.shape
    C = 3 * tok // (2 * E)
    H = E // 2
    NC, EC, HC = N * C, E * C, H * C
    block, ff = down_weight.shape[1:]
    parts = max(1, block // 256)
    by_dp = np.array([[j // C * EC + j % C] for j in range(NC)] * 2, np.int32)
    by_act = np.array([[i * N * HC + j // C * HC + j % C] for i in range(2) for j in range(NC)], np.int32)
    by_e = np.array(
        [[i // C % H * 2 * NC + i // HC * NC + i % C] for i in range(EC)], np.int32
    )
    dma = pltpu.SemaphoreType.DMA
    vmem = pl.BlockSpec(memory_space=pltpu.VMEM)
    down, hidden, probs = pl.pallas_call(
        functools.partial(kernel, E, N, C),
        out_shape=(
            jax.ShapeDtypeStruct((block, ff), F32),
            jax.ShapeDtypeStruct((EC, 2 * ff), BF16),
            jax.ShapeDtypeStruct((tok, 1), F32),
        ),
        in_specs=[vmem] * 8,
        out_specs=(vmem,) * 3,
        scratch_shapes=[
            pltpu.VMEM((parts, N, EC, block // parts), BF16),
            pltpu.VMEM((parts, N, EC, block // parts), BF16),
            pltpu.VMEM((2, N, HC, ff), BF16),
            pltpu.VMEM((H, 2, NC, ff), BF16),
            pltpu.VMEM((parts, H, 2, NC, block // parts), BF16),
            pltpu.VMEM((parts, H, 2, NC, block // parts), BF16),
            pltpu.VMEM((N, EC, ff), BF16),
            pltpu.VMEM((N, EC, ff), BF16),
            pltpu.VMEM((parts, block // parts, ff), BF16),
            pltpu.VMEM((parts, block // parts, ff), BF16),
            pltpu.VMEM((H, 8, EC), F32),
            pltpu.VMEM((tok, width), BF16),
            pltpu.VMEM((EC, tok), BF16),
            pltpu.VMEM((HC, ff), BF16),
            pltpu.VMEM((HC, ff), BF16),
            pltpu.VMEM((HC, ff), BF16),
            dma((parts, N)), dma((parts, N)), dma((2, N)), dma((2, N)), dma((parts, H)), dma((parts, H)),
            dma((N,)), dma((N,)), dma((parts,)), dma((parts,)), dma((H,)), dma((H,)),
            dma((2,)), dma((2,)),
        ],
        compiler_params=pltpu.CompilerParams(
            collective_id=0, has_side_effects=True, vmem_limit_bytes=56 * 2**20
        ),
        name="expert_backward",
    )(cotangent, router_probs, slot_ids, saved_hidden[0], down_weight[0], by_dp, by_act, by_e)
    return down[None], hidden[None], probs


def solution(mesh):
    placed = (
        P(("expert", "dp"), None),
        P(("expert", "dp"), None),
        P(("expert", "dp"), None),
        P("expert", "dp", None),
        P("expert", "dp", None),
    )
    return jax.shard_map(
        functools.partial(on_device, mesh.shape["expert"], mesh.shape["dp"]),
        mesh=mesh,
        in_specs=placed,
        out_specs=(P("expert", "dp", None), P("expert", "dp", None), P(("expert", "dp"), None)),
        check_vma=False,
    )
```
